32 devices in a mesh: seq: 8 (over z, y), head: 4 (over x, core).
Axes of the slice: x: 2, y: 2, z: 4, core: 2. Of those that a mesh axis runs over, the one named last changes fastest.
Arguments:
- queries: bfloat16 [1024, 4096], P('seq', 'head'), may hold values from -6 to 6
- key_rows: bfloat16 [1024, 4096], P('seq', 'head'), may hold values from -6 to 6
- value_rows: bfloat16 [1024, 4096], P('seq', 'head'), may hold values from -6 to 6
- log_decay: float32 [32, 1024], P('head', 'seq'), may hold values from -3 to 0
- init_state: float32 [32, 128, 128], P('head'), may hold values from -48 to 48
- attn_gain: float32 [4096], P('head'), may hold values from 0.1 to 1.9
- out_weight: bfloat16 [4096, 6144], P('head', 'seq'), may hold values from -0.09375 to 0.09375
- residual: bfloat16 [1024, 6144], P('seq', 'head'), may hold values from -13 to 13
- ffn_gain: float32 [6144], replicated, may hold values from 0.1 to 1.9
- router: float32 [6144, 8], replicated, may hold values from -0.078125 to 0.078125
- expert_ids: int32 [1024, 2], P('seq'), may hold values from 0 to 7, all different within a row; in each aligned block of 128 rows (0 to 127, 128 to 255, ...) at most 64 rows name the same one
- gate_weight: bfloat16 [8, 6144, 4608], P('seq', None, 'head'), may hold values from -0.078125 to 0.078125
- up_weight: bfloat16 [8, 6144, 4608], P('seq', None, 'head'), may hold values from -0.078125 to 0.078125
- down_weight: bfloat16 [8, 4608, 6144], P('seq', 'head'), may hold values from -0.09375 to 0.09375
Outputs:
- output: bfloat16 [1024, 6144], P('seq', 'head')
The draws below stay inside these ranges and needn't reach their ends.
Inputs may be any that keep to these rules, and one draw needn't show every extreme that they name: `expert_ids`: the two ids of a row differ. In each aligned block of 128 rows no expert is named more than 64 times, a bound that some block reaches.
All inputs are finite; a program needn't handle non-finite values.
Results may differ from the reference program's by a relative error of at most 0.018.
Values may be sent and summed in bfloat16 or wider, within the bound.
A program may use at most 128 MiB of HBM per device.

```python
import math
import jax
import jax.numpy as jnp
import numpy as np
from jax import lax

D = 6144
HEADS = 32
HEAD_DIM = 128
FF = 4608
TOK_DEV = 128
TOKENS = 1024
EXPERTS = 8
CAP = 64
N_SEQ = 8
N_HEAD = 4


def draw_log_decay(key, part):
    base = jax.random.fold_in(key, 101)
    k_fast, k_rate, k_slow, k_block, k_rough, k_spots, k_depth = jax.random.split(base, 7)
    fast_share = 0.5
    fast = jax.random.uniform(k_fast, (HEADS, 1)) < fast_share
    fast_rate = jnp.exp(jax.random.uniform(k_rate, (HEADS, 1), minval=math.log(2.5), maxval=math.log(4.0))) / TOK_DEV
    slow_rate = jnp.exp(jax.random.uniform(k_slow, (HEADS, 1), minval=math.log(0.5), maxval=math.log(1.0))) / TOKENS
    rate = jnp.where(fast, fast_rate, slow_rate)
    blocks = TOKENS // TOK_DEV
    block_factor = jnp.exp(jax.random.uniform(k_block, (HEADS, blocks, 1), minval=-0.35, maxval=0.35))
    rough = jax.random.uniform(k_rough, (HEADS, blocks, TOK_DEV), minval=0.5, maxval=1.5)
    steady = (rate[:, :, None] * block_factor * rough).reshape(HEADS, TOKENS)
    spots = jax.random.randint(k_spots, (3,), 0, TOKENS)
    struck = jnp.any(jnp.arange(TOKENS)[:, None] == spots[None, :], axis=1)
    depth = jax.random.uniform(k_depth, (HEADS, TOKENS), minval=math.log(0.55), maxval=math.log(0.8))
    return (jnp.where(struck[None, :], depth, 0.0) - steady).astype(jnp.float32)


def draw_residual(key, part):
    base = jax.random.fold_in(key, 202)
    k_main = jax.random.fold_in(base, 0)
    ramp = jnp.exp(jnp.arange(D, dtype=jnp.float32) / D * math.log(3.0))
    values = jnp.clip(jax.random.normal(k_main, (TOKENS, D)), -5.0, 5.0)
    return (values * ramp[None, :] * 0.6).astype(jnp.bfloat16)


def shard_levels(key, dims, pieces, smallest, top_value):
    def one(dim, parts):
        heights = jax.random.uniform(jax.random.fold_in(jax.random.fold_in(key, 6), dim), (parts,), jnp.float32, smallest / len(pieces), top_value / len(pieces))
        return jnp.repeat(jnp.exp(heights), dims[dim] // parts).reshape((-1,) + (1,) * (len(dims) - dim - 1))

    level = one(*pieces[0])
    for cut in pieces[1:]:
        level = level * one(*cut)
    return level


def deal_out(key, own, number, rows, amount, top, most, lean):
    order = jax.random.permutation(key, amount)
    crowded, usual = load_shares(amount, rows * top, most, lean, True), load_shares(amount, rows * top, most, lean, False)
    places = jnp.arange(amount)

    def named(sizes, turn):
        used = int((sizes > 0).sum())
        fixed = max(1, used // 4)
        moved = fixed + (places - fixed + turn * (used - fixed)) % max(1, amount - fixed)
        return jnp.zeros((amount,), jnp.int32).at[order[jnp.where(places < fixed, places, moved)]].set(jnp.asarray(sizes, jnp.int32))

    sizes = jnp.where(number % 4 == 0, named(crowded, number // 4), named(usual, number - number // 4 - 1))
    mixed = jax.random.permutation(jax.random.fold_in(own, 3), amount)
    giver, taker = mixed[0:amount // 2 * 2:2], mixed[1:amount // 2 * 2:2]
    margin = jnp.minimum(sizes[giver] - 1, most - sizes[taker]) // 2
    margin = jnp.where((giver == order[0]) | (taker == order[0]) | (sizes[taker] == 0), 0, jnp.maximum(margin, 0))
    moved = jax.random.randint(jax.random.fold_in(own, 4), (amount // 2,), 0, 1 << 20) % (margin + 1)
    sizes = sizes.at[giver].add(-moved).at[taker].add(moved)
    members = jnp.searchsorted(jnp.cumsum(sizes), jnp.arange(rows * top), side="right").astype(jnp.int32)
    listing = members.reshape(top, rows).T
    listing = listing[jax.random.permutation(jax.random.fold_in(own, 1), rows)]
    turn = jax.random.randint(jax.random.fold_in(own, 2), (rows, 1), 0, top)
    return jnp.take_along_axis(listing, (jnp.arange(top)[None, :] + turn) % top, axis=1)


def load_shares(amount, total, bound, lean, full):
    weights = [(1 << 20) // math.isqrt(standing ** lean) + 1 for standing in range(1, amount + 1)]
    largest = bound if full else min(bound, max(-(-total // amount), total * weights[0] // sum(weights)))
    least = 1 if total - largest >= amount - 1 else 0
    counts, rest = [largest] + [least] * (amount - 1), total - largest - least * (amount - 1)
    while rest > 0:
        movable = [i for i in range(1, amount) if counts[i] < largest] or [i for i in range(1, amount) if counts[i] < bound]
        mass, budget = sum([weights[i] for i in movable]), rest
        for i in movable:
            addition = min(bound - counts[i], max(1, budget * weights[i] // mass), rest)
            counts[i] = counts[i] + addition
            rest = rest - addition
    return np.array(counts)


def centred(key, shape, deviation, most, cuts=(), kind=jnp.bfloat16):
    array = deviation * jax.random.normal(key, shape, jnp.float32)
    if cuts:
        array = array * shard_levels(key, shape, cuts, -0.22, 0.18)
    return jnp.clip(array, -most, most).astype(kind)


def setup_inputs(seed: int = 0) -> dict:
    streams_of = jax.random.split(jax.random.key(seed), 15)
    queries = centred(streams_of[0], (TOKENS, HEADS * HEAD_DIM), 1.0, 6.0, ((0, 8), (1, 4)))
    key_rows = centred(streams_of[1], (TOKENS, HEADS * HEAD_DIM), 1.0, 6.0, ((0, 8), (1, 4)))
    value_rows = centred(streams_of[2], (TOKENS, HEADS * HEAD_DIM), 1.0, 6.0, ((0, 8), (1, 4)))
    log_decay = draw_log_decay(jax.random.fold_in(streams_of[14], 71), 0)
    init_state = centred(streams_of[4], (HEADS, HEAD_DIM, HEAD_DIM), 8.0, 48.0, ((0, 4),), jnp.float32)
    attn_gain = jnp.clip(1.0 + 0.18 * jax.random.normal(streams_of[5], (HEADS * HEAD_DIM,), jnp.float32), 0.1, 1.9)
    out_weight = centred(streams_of[6], (HEADS * HEAD_DIM, D), (HEADS * HEAD_DIM) ** -0.5, 0.09375, ((0, 4), (1, 8)))
    residual = draw_residual(jax.random.fold_in(streams_of[14], 71), 0)
    ffn_gain = jnp.clip(1.0 + 0.18 * jax.random.normal(streams_of[8], (D,), jnp.float32), 0.1, 1.9)
    router = centred(streams_of[9], (D, EXPERTS), D ** -0.5, 0.078125, (), jnp.float32)
    expert_ids_keys = jax.random.split(jax.random.fold_in(streams_of[10], 1), TOKENS // TOK_DEV)
    expert_ids_turns = jax.random.permutation(jax.random.fold_in(streams_of[10], 3), TOKENS // TOK_DEV)
    expert_ids = jax.vmap(lambda own, number: deal_out(jax.random.fold_in(streams_of[10], 2), own, number, TOK_DEV, EXPERTS, 2, CAP, 2))(expert_ids_keys, expert_ids_turns).reshape((TOKENS, 2))
    gate_weight = centred(streams_of[11], (EXPERTS, D, FF), D ** -0.5, 0.078125, ((0, 8), (2, 4)))
    up_weight = centred(streams_of[12], (EXPERTS, D, FF), D ** -0.5, 0.078125, ((0, 8), (2, 4)))
    down_weight = centred(streams_of[13], (EXPERTS, FF, D), FF ** -0.5, 0.09375, ((0, 8), (1, 4)))
    return {"queries": queries, "key_rows": key_rows, "value_rows": value_rows, "log_decay": log_decay, "init_state": init_state, "attn_gain": attn_gain, "out_weight": out_weight, "residual": residual, "ffn_gain": ffn_gain, "router": router, "expert_ids": expert_ids, "gate_weight": gate_weight, "up_weight": up_weight, "down_weight": down_weight}


epsilon = 1e-06
highest = lax.Precision.HIGHEST

def block_attend(query_block, key_block, value_block, cumulative, entering):
    length = cumulative.shape[1]
    causal = jnp.arange(length)[:, None] >= jnp.arange(length)[None, :]
    spread = jnp.where(causal[None], cumulative[:, :, None] - cumulative[:, None, :], 0.0)
    fading = jnp.where(causal[None], jnp.exp(spread), 0.0)
    scores = jnp.einsum('thd,shd->hts', query_block.astype(jnp.float32), key_block.astype(jnp.float32), precision=highest)
    weights = (fading * scores).astype(jnp.bfloat16)
    within = jnp.einsum('hts,shd->thd', weights.astype(jnp.float32), value_block.astype(jnp.float32), precision=highest)
    carried = jnp.einsum('thd,hde->the', query_block.astype(jnp.float32), entering, precision=highest)
    return within + jnp.exp(cumulative).T[:, :, None] * carried

def block_state(key_block, value_block, cumulative):
    remain = jnp.exp(cumulative[:, -1:] - cumulative)
    return jnp.einsum('shd,hs,she->hde', key_block.astype(jnp.float32), remain, value_block.astype(jnp.float32), precision=highest)

def reference(queries, key_rows, value_rows, log_decay, init_state, attn_gain, out_weight, residual, ffn_gain, router, expert_ids, gate_weight, up_weight, down_weight):
    blocks = TOKENS // TOK_DEV
    shaped = (blocks, TOK_DEV, HEADS, HEAD_DIM)
    query_blocks = queries.reshape(shaped)
    key_blocks = key_rows.reshape(shaped)
    value_blocks = value_rows.reshape(shaped)
    decay_blocks = log_decay.reshape(HEADS, blocks, TOK_DEV).transpose(1, 0, 2)

    def advance(carried_state, inputs):
        query_block, key_block, value_block, decay_block = inputs
        cumulative = jnp.cumsum(decay_block, axis=1)
        attended = block_attend(query_block, key_block, value_block, cumulative, carried_state)
        carried_state = jnp.exp(cumulative[:, -1])[:, None, None] * carried_state + block_state(key_block, value_block, cumulative)
        return (carried_state, attended)
    final_state, attended = lax.scan(advance, init_state, (query_blocks, key_blocks, value_blocks, decay_blocks))
    attended = attended.reshape(TOKENS, HEADS, HEAD_DIM)
    inverse = lax.rsqrt(lax.optimization_barrier(jnp.mean(attended * attended, axis=-1, keepdims=True)) + epsilon)
    attn_rows = (attended * inverse * attn_gain.reshape(HEADS, HEAD_DIM)).reshape(TOKENS, HEADS * HEAD_DIM).astype(jnp.bfloat16)
    stream = residual.astype(jnp.float32) + jnp.dot(attn_rows, out_weight, preferred_element_type=jnp.float32)
    inverse_rms = lax.rsqrt(lax.optimization_barrier(jnp.mean(stream * stream, axis=-1, keepdims=True)) + epsilon)
    normed = stream * inverse_rms * ffn_gain
    logits = jnp.dot(normed, router, precision=highest)
    experts = router.shape[1]
    chosen_hits = expert_ids[:, :, None] == jnp.arange(experts, dtype=jnp.int32)[None, None, :]
    chosen = lax.optimization_barrier(jnp.sum(jnp.where(chosen_hits, logits[:, None, :], 0.0), axis=-1))
    gate_share = jax.nn.sigmoid(chosen - chosen[:, ::-1])
    expert_in = normed.astype(jnp.bfloat16)
    room_rows = N_SEQ * CAP
    flat_ids = expert_ids.reshape(-1).astype(jnp.int32)
    matches = (flat_ids[:, None] == jnp.arange(experts, dtype=jnp.int32)[None, :]).astype(jnp.int32)
    position = lax.optimization_barrier(jnp.sum(jnp.cumsum(matches, axis=0) * matches, axis=1)) - 1
    slot_index = (flat_ids * room_rows + position).astype(jnp.int32)
    token_of = jnp.arange(2 * TOKENS, dtype=jnp.int32) // 2
    source = jnp.zeros((experts * room_rows,), jnp.int32).at[slot_index].set(token_of)
    filled = jnp.zeros((experts * room_rows,), jnp.int32).at[slot_index].set(1)
    grouped = jnp.where(filled[:, None] > 0, expert_in[source], jnp.zeros((), jnp.bfloat16)).reshape(experts, room_rows, D)
    piece_width = FF // N_HEAD

    def one_expert(inputs):
        rows_in, gate_matrix, up_matrix, down_matrix = inputs
        gate_act = jnp.dot(rows_in, gate_matrix, preferred_element_type=jnp.float32)
        up_act = jnp.dot(rows_in, up_matrix, preferred_element_type=jnp.float32)
        hidden = (jax.nn.silu(gate_act) * up_act).astype(jnp.bfloat16)
        total_out = jnp.zeros((room_rows, D), jnp.float32)
        for portion in range(N_HEAD):
            section = hidden[:, portion * piece_width:(portion + 1) * piece_width]
            rows_down = down_matrix[portion * piece_width:(portion + 1) * piece_width]
            partial_value = jnp.dot(section, rows_down, preferred_element_type=jnp.float32).astype(jnp.bfloat16)
            total_out = total_out + lax.optimization_barrier(partial_value).astype(jnp.float32)
        return total_out.astype(jnp.bfloat16)
    expert_out = lax.map(one_expert, (grouped, gate_weight, up_weight, down_weight))
    picked = expert_out.reshape(experts * room_rows, D)[slot_index].reshape(TOKENS, 2, D).astype(jnp.float32)
    return (stream + lax.optimization_barrier(jnp.sum(gate_share[:, :, None] * picked, axis=1))).astype(jnp.bfloat16)
```

```python
import jax
import jax.numpy as jnp
from jax import lax
from jax.sharding import PartitionSpec as P

D = 6144
HEAD_DIM = 128


epsilon = 1e-06
highest = lax.Precision.HIGHEST


def prefix(x, axis, combine, identity):
    size, place = (lax.axis_size(axis), lax.axis_index(axis))
    everything = jax.tree.map(
        lambda part, kind: lax.all_gather(part.astype(kind), axis), x, (jnp.bfloat16, jnp.bfloat16)
    )
    start = jax.tree.map(
        lambda part, zero: jnp.broadcast_to(jnp.asarray(zero, part.dtype), part.shape), x, identity
    )

    def turn(k, before):
        reached = k < place
        new = combine(
            before, jax.tree.map(lambda part, own: part[k].astype(own.dtype), everything, x)
        )
        return jax.tree.map(lambda a, b: jnp.where(reached, a, b), new, before)

    return lax.fori_loop(0, size, turn, start)


def block_attend(query_block, key_block, value_block, cumulative, entering):
    length = cumulative.shape[1]
    causal = jnp.arange(length)[:, None] >= jnp.arange(length)[None, :]
    spread = jnp.where(causal[None], cumulative[:, :, None] - cumulative[:, None, :], 0.0)
    fading = jnp.where(causal[None], jnp.exp(spread), 0.0)
    scores = jnp.einsum("thd,shd->hts", query_block, key_block, preferred_element_type=jnp.float32)
    weights = (fading * scores).astype(jnp.bfloat16)
    within = jnp.einsum("hts,shd->thd", weights, value_block, preferred_element_type=jnp.float32)
    carried = jnp.einsum(
        "thd,hde->the", query_block.astype(jnp.float32), entering, precision=highest
    )
    return within + jnp.exp(cumulative).T[:, :, None] * carried


def block_state(key_block, value_block, cumulative):
    remain = jnp.exp(cumulative[:, -1:] - cumulative)
    return jnp.einsum(
        "shd,hs,she->hde",
        key_block.astype(jnp.float32),
        remain,
        value_block.astype(jnp.float32),
        precision=highest,
    )


def join_states(earlier, latter):
    return (earlier[0] + latter[0], jnp.exp(latter[0])[:, None, None] * earlier[1] + latter[1])


def on_device(
    queries,
    key_rows,
    value_rows,
    log_decay,
    init_state,
    attn_gain,
    out_weight,
    residual,
    ffn_gain,
    router,
    expert_ids,
    gate_weight,
    up_weight,
    down_weight,
):
    tokens_here = queries.shape[0]
    heads_here = log_decay.shape[0]
    shaped = (tokens_here, heads_here, HEAD_DIM)
    query_heads = queries.reshape(shaped)
    key_heads = key_rows.reshape(shaped)
    value_heads = value_rows.reshape(shaped)
    upto = jnp.arange(tokens_here)[:, None] >= jnp.arange(tokens_here)[None, :]
    cumulative = jnp.sum(jnp.where(upto[None], log_decay[:, None, :], 0.0), axis=-1)
    block_decay = cumulative[:, -1]
    local_state = block_state(key_heads, value_heads, cumulative)
    identity = (jnp.zeros_like(block_decay), jnp.zeros_like(local_state))
    prior_decay, prior_state = prefix((block_decay, local_state), "seq", join_states, identity)
    entering = jnp.exp(prior_decay)[:, None, None] * init_state + prior_state
    attended = block_attend(query_heads, key_heads, value_heads, cumulative, entering)
    inverse = lax.rsqrt(jnp.mean(attended * attended, axis=-1, keepdims=True) + epsilon)
    attn_rows = (
        (attended * inverse * attn_gain.reshape(heads_here, HEAD_DIM))
        .reshape(tokens_here, heads_here * HEAD_DIM)
        .astype(jnp.bfloat16)
    )
    projected = jnp.dot(
        attn_rows,
        lax.all_gather(out_weight, "seq", axis=1, tiled=True),
        preferred_element_type=jnp.float32,
    )
    width_here = residual.shape[1]
    first_column = lax.axis_index("head") * width_here
    own_columns = lax.dynamic_slice_in_dim(
        projected, first_column, width_here, 1
    ) + residual.astype(jnp.float32)
    projected = lax.dynamic_update_slice_in_dim(projected, own_columns, first_column, 1)
    experts = router.shape[1]
    stream_here = lax.psum_scatter(
        projected.astype(jnp.bfloat16), "head", scatter_dimension=1, tiled=True
    ).astype(jnp.float32)
    gain_here = lax.dynamic_slice_in_dim(ffn_gain, first_column, width_here, 0)
    router_here = lax.dynamic_slice_in_dim(router, first_column, width_here, 0)
    weighted = stream_here * gain_here
    squares, partial_logits = lax.psum(
        (
            jnp.sum(stream_here * stream_here, axis=-1),
            jnp.dot(weighted, router_here, precision=highest),
        ),
        "head",
    )
    inverse_rms = lax.rsqrt(squares / D + epsilon)[:, None]
    normed = weighted * inverse_rms
    logits = partial_logits * inverse_rms
    expert_in = normed.astype(jnp.bfloat16)
    matches = expert_ids[:, :, None] == jnp.arange(experts)[None, None, :]
    chosen = jnp.sum(jnp.where(matches, logits[:, None, :], 0.0), axis=-1)
    gate_share = jax.nn.sigmoid(chosen - chosen[:, ::-1])
    capacity = 4 * tokens_here // experts
    flat_ids = expert_ids.reshape(-1)
    order = jnp.arange(tokens_here * 2)
    ahead = (flat_ids[None, :] == flat_ids[:, None]) & (order[None, :] < order[:, None])
    position = jnp.sum(ahead.astype(jnp.int32), axis=1)
    slot_index = flat_ids * capacity + position
    target = slot_index[None, :] == jnp.arange(experts * capacity)[:, None]
    source = jnp.sum(jnp.where(target, jnp.arange(tokens_here * 2)[None, :] // 2, 0), axis=1)
    filled = jnp.any(target, axis=1)
    outgoing = jnp.where(filled[:, None], expert_in[source], jnp.zeros((), jnp.bfloat16)).reshape(
        experts, capacity, -1
    )
    gate_here = gate_weight[0]
    up_here = up_weight[0]
    down_here = down_weight[0]
    arrived = lax.all_to_all(outgoing, "seq", split_axis=0, concat_axis=0, tiled=True)
    sources, slot_count, columns = arrived.shape
    flat_rows = arrived.reshape(sources * slot_count, columns)
    portion = lax.all_gather(flat_rows, "head", axis=1, tiled=True)
    gate_act = jnp.dot(portion, gate_here, preferred_element_type=jnp.float32)
    up_act = jnp.dot(portion, up_here, preferred_element_type=jnp.float32)
    hidden = (jax.nn.silu(gate_act) * up_act).astype(jnp.bfloat16)
    partial_value = jnp.dot(hidden, down_here, preferred_element_type=jnp.float32)
    summed = lax.psum_scatter(
        partial_value.astype(jnp.bfloat16), "head", scatter_dimension=1, tiled=True
    )
    returning = summed.reshape(sources, slot_count, -1)
    returned = lax.all_to_all(returning, "seq", split_axis=0, concat_axis=0, tiled=True)
    flat_back = returned.reshape(experts * capacity, -1)
    picked = flat_back[slot_index].reshape(tokens_here, 2, -1).astype(jnp.float32)
    mixture = jnp.sum(gate_share[:, :, None] * picked, axis=1)
    return (stream_here + mixture).astype(jnp.bfloat16)


def solution(mesh):
    return jax.shard_map(
        on_device,
        mesh=mesh,
        in_specs=(
            P("seq", "head"),
            P("seq", "head"),
            P("seq", "head"),
            P("head", "seq"),
            P("head", None, None),
            P("head"),
            P("head", "seq"),
            P("seq", "head"),
            P(),
            P(),
            P("seq", None),
            P("seq", None, "head"),
            P("seq", None, "head"),
            P("seq", "head", None),
        ),
        out_specs=P("seq", "head"),
        check_vma=False,
    )
```

```python
import jax
import jax.numpy as jnp
from jax import lax
from jax.sharding import PartitionSpec as P

D = 6144
HEAD_DIM = 128


epsilon = 1e-06
highest = lax.Precision.HIGHEST


def prefix(x, axis, combine, identity):
    size, place = (lax.axis_size(axis), lax.axis_index(axis))
    everything = jax.tree.map(
        lambda part, kind: lax.all_gather(part.astype(kind), axis), x, (jnp.bfloat16, jnp.bfloat16)
    )
    start = jax.tree.map(
        lambda part, zero: jnp.broadcast_to(jnp.asarray(zero, part.dtype), part.shape), x, identity
    )

    def turn(k, before):
        reached = k < place
        new = combine(
            before, jax.tree.map(lambda part, own: part[k].astype(own.dtype), everything, x)
        )
        return jax.tree.map(lambda a, b: jnp.where(reached, a, b), new, before)

    return lax.fori_loop(0, size, turn, start)


def block_attend(query_block, key_block, value_block, cumulative, entering):
    length = cumulative.shape[1]
    causal = jnp.arange(length)[:, None] >= jnp.arange(length)[None, :]
    spread = jnp.where(causal[None], cumulative[:, :, None] - cumulative[:, None, :], 0.0)
    fading = jnp.where(causal[None], jnp.exp(spread), 0.0)
    scores = jnp.einsum("thd,shd->hts", query_block, key_block, preferred_element_type=jnp.float32)
    weights = (fading * scores).astype(jnp.bfloat16)
    within = jnp.einsum("hts,shd->thd", weights, value_block, preferred_element_type=jnp.float32)
    carried = jnp.einsum(
        "thd,hde->the", query_block.astype(jnp.float32), entering, precision=highest
    )
    return within + jnp.exp(cumulative).T[:, :, None] * carried


def block_state(key_block, value_block, cumulative):
    remain = jnp.exp(cumulative[:, -1:] - cumulative)
    return jnp.einsum(
        "shd,hs,she->hde",
        key_block.astype(jnp.float32),
        remain,
        value_block.astype(jnp.float32),
        precision=highest,
    )


def join_states(earlier, latter):
    return (earlier[0] + latter[0], jnp.exp(latter[0])[:, None, None] * earlier[1] + latter[1])


def project(attn_rows, out_weight):
    seq_size, head_size = (lax.axis_size("seq"), lax.axis_size("head"))
    place = lax.axis_index("seq")
    tokens_here = attn_rows.shape[0]
    ratio = seq_size // head_size
    all_rows = lax.all_gather(attn_rows, "seq", axis=0, tiled=True)
    products = jnp.dot(all_rows, out_weight, preferred_element_type=jnp.float32)
    sums = lax.psum_scatter(
        products.astype(jnp.bfloat16), "head", scatter_dimension=0, tiled=True
    ).reshape(ratio, tokens_here, -1)
    landed = []
    for turn in range(ratio):
        pairs = [
            (s * head_size + h, (ratio * h + (s + turn) % ratio) * head_size + s // ratio)
            for s in range(seq_size)
            for h in range(head_size)
        ]
        part = lax.dynamic_index_in_dim(sums, (place + turn) % ratio, 0, keepdims=False)
        landed.append(lax.ppermute(part, ("seq", "head"), pairs))
    landed = jnp.stack(landed)
    return jnp.concatenate(
        [
            lax.dynamic_index_in_dim(landed, (place - b) % ratio, 0, keepdims=False)
            for b in range(ratio)
        ],
        axis=1,
    )


def on_device(
    queries,
    key_rows,
    value_rows,
    log_decay,
    init_state,
    attn_gain,
    out_weight,
    residual,
    ffn_gain,
    router,
    expert_ids,
    gate_weight,
    up_weight,
    down_weight,
):
    tokens_here = queries.shape[0]
    heads_here = log_decay.shape[0]
    shaped = (tokens_here, heads_here, HEAD_DIM)
    query_heads = queries.reshape(shaped)
    key_heads = key_rows.reshape(shaped)
    value_heads = value_rows.reshape(shaped)
    upto = jnp.arange(tokens_here)[:, None] >= jnp.arange(tokens_here)[None, :]
    cumulative = jnp.sum(jnp.where(upto[None], log_decay[:, None, :], 0.0), axis=-1)
    block_decay = cumulative[:, -1]
    local_state = block_state(key_heads, value_heads, cumulative)
    identity = (jnp.zeros_like(block_decay), jnp.zeros_like(local_state))
    prior_decay, prior_state = prefix((block_decay, local_state), "seq", join_states, identity)
    entering = jnp.exp(prior_decay)[:, None, None] * init_state + prior_state
    attended = block_attend(query_heads, key_heads, value_heads, cumulative, entering)
    inverse = lax.rsqrt(jnp.mean(attended * attended, axis=-1, keepdims=True) + epsilon)
    attn_rows = (
        (attended * inverse * attn_gain.reshape(heads_here, HEAD_DIM))
        .reshape(tokens_here, heads_here * HEAD_DIM)
        .astype(jnp.bfloat16)
    )
    width_here = residual.shape[1]
    first_column = lax.axis_index("head") * width_here
    experts = router.shape[1]
    stream_here = residual.astype(jnp.float32) + project(attn_rows, out_weight).astype(jnp.float32)
    gain_here = lax.dynamic_slice_in_dim(ffn_gain, first_column, width_here, 0)
    router_here = lax.dynamic_slice_in_dim(router, first_column, width_here, 0)
    weighted = stream_here * gain_here
    squares, partial_logits = lax.psum(
        (
            jnp.sum(stream_here * stream_here, axis=-1),
            jnp.dot(weighted, router_here, precision=highest),
        ),
        "head",
    )
    inverse_rms = lax.rsqrt(squares / D + epsilon)[:, None]
    normed = weighted * inverse_rms
    logits = partial_logits * inverse_rms
    expert_in = normed.astype(jnp.bfloat16)
    matches = expert_ids[:, :, None] == jnp.arange(experts)[None, None, :]
    chosen = jnp.sum(jnp.where(matches, logits[:, None, :], 0.0), axis=-1)
    gate_share = jax.nn.sigmoid(chosen - chosen[:, ::-1])
    capacity = 4 * tokens_here // experts
    flat_ids = expert_ids.reshape(-1)
    order = jnp.arange(tokens_here * 2)
    ahead = (flat_ids[None, :] == flat_ids[:, None]) & (order[None, :] < order[:, None])
    position = jnp.sum(ahead.astype(jnp.int32), axis=1)
    slot_index = flat_ids * capacity + position
    target = slot_index[None, :] == jnp.arange(experts * capacity)[:, None]
    source = jnp.sum(jnp.where(target, jnp.arange(tokens_here * 2)[None, :] // 2, 0), axis=1)
    filled = jnp.any(target, axis=1)
    outgoing = jnp.where(filled[:, None], expert_in[source], jnp.zeros((), jnp.bfloat16)).reshape(
        experts, capacity, -1
    )
    gate_here = gate_weight[0]
    up_here = up_weight[0]
    down_here = down_weight[0]
    arrived = lax.all_to_all(outgoing, "seq", split_axis=0, concat_axis=0, tiled=True)
    sources, slot_count, columns = arrived.shape
    flat_rows = arrived.reshape(sources * slot_count, columns)
    portion = lax.all_gather(flat_rows, "head", axis=1, tiled=True)
    gate_act = jnp.dot(portion, gate_here, preferred_element_type=jnp.float32)
    up_act = jnp.dot(portion, up_here, preferred_element_type=jnp.float32)
    hidden = (jax.nn.silu(gate_act) * up_act).astype(jnp.bfloat16)
    partial_value = jnp.dot(hidden, down_here, preferred_element_type=jnp.float32)
    summed = lax.psum_scatter(
        partial_value.astype(jnp.bfloat16), "head", scatter_dimension=1, tiled=True
    )
    returning = summed.reshape(sources, slot_count, -1)
    returned = lax.all_to_all(returning, "seq", split_axis=0, concat_axis=0, tiled=True)
    flat_back = returned.reshape(experts * capacity, -1)
    picked = flat_back[slot_index].reshape(tokens_here, 2, -1).astype(jnp.float32)
    mixture = jnp.sum(gate_share[:, :, None] * picked, axis=1)
    return (stream_here + mixture).astype(jnp.bfloat16)


def solution(mesh):
    return jax.shard_map(
        on_device,
        mesh=mesh,
        in_specs=(
            P("seq", "head"),
            P("seq", "head"),
            P("seq", "head"),
            P("head", "seq"),
            P("head", None, None),
            P("head"),
            P("head", "seq"),
            P("seq", "head"),
            P(),
            P(),
            P("seq", None),
            P("seq", None, "head"),
            P("seq", None, "head"),
            P("seq", "head", None),
        ),
        out_specs=P("seq", "head"),
        check_vma=False,
    )
```

```python
import jax
import jax.numpy as jnp
from jax import lax
from jax.sharding import PartitionSpec as P

D = 6144
HEAD_DIM = 128
CHUNKS = 2


epsilon = 1e-06
highest = lax.Precision.HIGHEST


def prefix(x, axis, combine, identity):
    size, place = (lax.axis_size(axis), lax.axis_index(axis))
    everything = jax.tree.map(
        lambda part, kind: lax.all_gather(part.astype(kind), axis), x, (jnp.bfloat16, jnp.bfloat16)
    )
    start = jax.tree.map(
        lambda part, zero: jnp.broadcast_to(jnp.asarray(zero, part.dtype), part.shape), x, identity
    )

    def turn(k, before):
        reached = k < place
        new = combine(
            before, jax.tree.map(lambda part, own: part[k].astype(own.dtype), everything, x)
        )
        return jax.tree.map(lambda a, b: jnp.where(reached, a, b), new, before)

    return lax.fori_loop(0, size, turn, start)


def block_attend(query_block, key_block, value_block, cumulative, entering):
    length = cumulative.shape[1]
    causal = jnp.arange(length)[:, None] >= jnp.arange(length)[None, :]
    spread = jnp.where(causal[None], cumulative[:, :, None] - cumulative[:, None, :], 0.0)
    fading = jnp.where(causal[None], jnp.exp(spread), 0.0)
    scores = jnp.einsum("thd,shd->hts", query_block, key_block, preferred_element_type=jnp.float32)
    weights = (fading * scores).astype(jnp.bfloat16)
    within = jnp.einsum("hts,shd->thd", weights, value_block, preferred_element_type=jnp.float32)
    carried = jnp.einsum(
        "thd,hde->the", query_block.astype(jnp.float32), entering, precision=highest
    )
    return within + jnp.exp(cumulative).T[:, :, None] * carried


def block_state(key_block, value_block, cumulative):
    remain = jnp.exp(cumulative[:, -1:] - cumulative)
    return jnp.einsum(
        "shd,hs,she->hde",
        key_block.astype(jnp.float32),
        remain,
        value_block.astype(jnp.float32),
        precision=highest,
    )


def join_states(earlier, latter):
    return (earlier[0] + latter[0], jnp.exp(latter[0])[:, None, None] * earlier[1] + latter[1])


def project(attn_rows, out_weight):
    seq_size, head_size = (lax.axis_size("seq"), lax.axis_size("head"))
    place = lax.axis_index("seq")
    tokens_here = attn_rows.shape[0]
    ratio = seq_size // head_size
    all_rows = lax.all_gather(attn_rows, "seq", axis=0, tiled=True)
    products = jnp.dot(all_rows, out_weight, preferred_element_type=jnp.float32)
    sums = lax.psum_scatter(
        products.astype(jnp.bfloat16), "head", scatter_dimension=0, tiled=True
    ).reshape(ratio, tokens_here, -1)
    landed = []
    for turn in range(ratio):
        pairs = [
            (s * head_size + h, (ratio * h + (s + turn) % ratio) * head_size + s // ratio)
            for s in range(seq_size)
            for h in range(head_size)
        ]
        part = lax.dynamic_index_in_dim(sums, (place + turn) % ratio, 0, keepdims=False)
        landed.append(lax.ppermute(part, ("seq", "head"), pairs))
    landed = jnp.stack(landed)
    return jnp.concatenate(
        [
            lax.dynamic_index_in_dim(landed, (place - b) % ratio, 0, keepdims=False)
            for b in range(ratio)
        ],
        axis=1,
    )


def on_device(
    queries,
    key_rows,
    value_rows,
    log_decay,
    init_state,
    attn_gain,
    out_weight,
    residual,
    ffn_gain,
    router,
    expert_ids,
    gate_weight,
    up_weight,
    down_weight,
):
    tokens_here = queries.shape[0]
    heads_here = log_decay.shape[0]
    shaped = (tokens_here, heads_here, HEAD_DIM)
    query_heads = queries.reshape(shaped)
    key_heads = key_rows.reshape(shaped)
    value_heads = value_rows.reshape(shaped)
    upto = jnp.arange(tokens_here)[:, None] >= jnp.arange(tokens_here)[None, :]
    cumulative = jnp.sum(jnp.where(upto[None], log_decay[:, None, :], 0.0), axis=-1)
    block_decay = cumulative[:, -1]
    local_state = block_state(key_heads, value_heads, cumulative)
    identity = (jnp.zeros_like(block_decay), jnp.zeros_like(local_state))
    prior_decay, prior_state = prefix((block_decay, local_state), "seq", join_states, identity)
    entering = jnp.exp(prior_decay)[:, None, None] * init_state + prior_state
    attended = block_attend(query_heads, key_heads, value_heads, cumulative, entering)
    inverse = lax.rsqrt(jnp.mean(attended * attended, axis=-1, keepdims=True) + epsilon)
    attn_rows = (
        (attended * inverse * attn_gain.reshape(heads_here, HEAD_DIM))
        .reshape(tokens_here, heads_here * HEAD_DIM)
        .astype(jnp.bfloat16)
    )
    width_here = residual.shape[1]
    first_column = lax.axis_index("head") * width_here
    experts = router.shape[1]
    stream_here = residual.astype(jnp.float32) + project(attn_rows, out_weight).astype(jnp.float32)
    gain_here = lax.dynamic_slice_in_dim(ffn_gain, first_column, width_here, 0)
    router_here = lax.dynamic_slice_in_dim(router, first_column, width_here, 0)
    weighted = stream_here * gain_here
    squares, partial_logits = lax.psum(
        (
            jnp.sum(stream_here * stream_here, axis=-1),
            jnp.dot(weighted, router_here, precision=highest),
        ),
        "head",
    )
    inverse_rms = lax.rsqrt(squares / D + epsilon)[:, None]
    normed = weighted * inverse_rms
    logits = partial_logits * inverse_rms
    expert_in = normed.astype(jnp.bfloat16)
    matches = expert_ids[:, :, None] == jnp.arange(experts)[None, None, :]
    chosen = jnp.sum(jnp.where(matches, logits[:, None, :], 0.0), axis=-1)
    gate_share = jax.nn.sigmoid(chosen - chosen[:, ::-1])
    capacity = 4 * tokens_here // experts
    flat_ids = expert_ids.reshape(-1)
    order = jnp.arange(tokens_here * 2)
    ahead = (flat_ids[None, :] == flat_ids[:, None]) & (order[None, :] < order[:, None])
    position = jnp.sum(ahead.astype(jnp.int32), axis=1)
    slot_index = flat_ids * capacity + position
    target = slot_index[None, :] == jnp.arange(experts * capacity)[:, None]
    source = jnp.sum(jnp.where(target, jnp.arange(tokens_here * 2)[None, :] // 2, 0), axis=1)
    filled = jnp.any(target, axis=1)
    outgoing = jnp.where(filled[:, None], expert_in[source], jnp.zeros((), jnp.bfloat16)).reshape(
        experts, capacity, -1
    )
    gate_here = gate_weight[0]
    up_here = up_weight[0]
    down_here = down_weight[0]
    chunk = capacity // CHUNKS
    arrivals = [
        lax.all_to_all(
            outgoing[:, c * chunk : (c + 1) * chunk],
            "seq",
            split_axis=0,
            concat_axis=0,
            tiled=True,
        )
        for c in range(CHUNKS)
    ]
    results = []
    for arrived in arrivals:
        flat_rows = arrived.reshape(experts * chunk, -1)
        portion = lax.all_gather(flat_rows, "head", axis=1, tiled=True)
        gate_act = jnp.dot(portion, gate_here, preferred_element_type=jnp.float32)
        up_act = jnp.dot(portion, up_here, preferred_element_type=jnp.float32)
        hidden = (jax.nn.silu(gate_act) * up_act).astype(jnp.bfloat16)
        partial_value = jnp.dot(hidden, down_here, preferred_element_type=jnp.float32)
        summed = lax.psum_scatter(
            partial_value.astype(jnp.bfloat16), "head", scatter_dimension=1, tiled=True
        )
        returning = summed.reshape(experts, chunk, -1)
        results.append(
            lax.all_to_all(returning, "seq", split_axis=0, concat_axis=0, tiled=True)
        )
    returned = jnp.concatenate(results, axis=1)
    flat_back = returned.reshape(experts * capacity, -1)
    picked = flat_back[slot_index].reshape(tokens_here, 2, -1).astype(jnp.float32)
    mixture = jnp.sum(gate_share[:, :, None] * picked, axis=1)
    return (stream_here + mixture).astype(jnp.bfloat16)


def solution(mesh):
    return jax.shard_map(
        on_device,
        mesh=mesh,
        in_specs=(
            P("seq", "head"),
            P("seq", "head"),
            P("seq", "head"),
            P("head", "seq"),
            P("head", None, None),
            P("head"),
            P("head", "seq"),
            P("seq", "head"),
            P(),
            P(),
            P("seq", None),
            P("seq", None, "head"),
            P("seq", None, "head"),
            P("seq", "head", None),
        ),
        out_specs=P("seq", "head"),
        check_vma=False,
    )
```

```python
import jax
import jax.numpy as jnp
from jax import lax
from jax.sharding import PartitionSpec as P

D = 6144
HEAD_DIM = 128
CHUNKS = 2


epsilon = 1e-06
highest = lax.Precision.HIGHEST


def shift(x, turn, size, cyclic):
    pairs = [(s, (s + turn) % size) for s in range(size) if cyclic or s + turn < size]
    return lax.ppermute(x, "seq", pairs)


def prior_blocks(block_decay, local_state):
    size = lax.axis_size("seq")
    heads, rows, width = local_state.shape
    coarse = lax.reduce_precision(block_decay, 8, 7)
    terms = jnp.concatenate([coarse, block_decay - coarse])
    packed = jnp.concatenate(
        [
            local_state.reshape(heads * rows, width).astype(jnp.bfloat16),
            jnp.broadcast_to(terms[:, None], (2 * heads, width)).astype(jnp.bfloat16),
        ]
    )
    landed = [shift(packed, turn, size, False) for turn in range(1, size)]
    decay = jnp.zeros_like(block_decay)
    state = jnp.zeros_like(local_state)
    for block in landed:
        arrived = block[: heads * rows].astype(jnp.float32).reshape(heads, rows, width)
        parts = block[heads * rows :, 0].astype(jnp.float32)
        state = state + jnp.exp(decay)[:, None, None] * arrived
        decay = decay + (parts[:heads] + parts[heads:])
    return decay, state


def block_attend(query_block, key_block, value_block, cumulative, entering):
    length = cumulative.shape[1]
    causal = jnp.arange(length)[:, None] >= jnp.arange(length)[None, :]
    spread = jnp.where(causal[None], cumulative[:, :, None] - cumulative[:, None, :], 0.0)
    fading = jnp.where(causal[None], jnp.exp(spread), 0.0)
    scores = jnp.einsum("thd,shd->hts", query_block, key_block, preferred_element_type=jnp.float32)
    weights = (fading * scores).astype(jnp.bfloat16)
    within = jnp.einsum("hts,shd->thd", weights, value_block, preferred_element_type=jnp.float32)
    carried = jnp.einsum(
        "thd,hde->the", query_block.astype(jnp.float32), entering, precision=highest
    )
    return within + jnp.exp(cumulative).T[:, :, None] * carried


def block_state(key_block, value_block, cumulative):
    remain = jnp.exp(cumulative[:, -1:] - cumulative)
    return jnp.einsum(
        "shd,hs,she->hde",
        key_block.astype(jnp.float32),
        remain,
        value_block.astype(jnp.float32),
        precision=highest,
    )


def project(attn_rows, out_weight):
    seq_size, head_size = (lax.axis_size("seq"), lax.axis_size("head"))
    place = lax.axis_index("seq")
    tokens_here = attn_rows.shape[0]
    ratio = seq_size // head_size
    blocks = [attn_rows] + [shift(attn_rows, k, seq_size, True) for k in range(1, seq_size)]
    products = jnp.concatenate(
        [
            jnp.dot(rows, out_weight, preferred_element_type=jnp.float32).astype(jnp.bfloat16)
            for rows in blocks
        ]
    )
    sums = lax.psum_scatter(products, "head", scatter_dimension=0, tiled=True).reshape(
        ratio, tokens_here, -1
    )
    landed = []
    for turn in range(ratio):
        pairs = [
            (s * head_size + h, (s - ratio * h - turn) % seq_size * head_size + s // ratio)
            for s in range(seq_size)
            for h in range(head_size)
        ]
        landed.append(lax.ppermute(sums[turn], ("seq", "head"), pairs))
    landed = jnp.stack(landed)
    return jnp.concatenate(
        [
            lax.dynamic_index_in_dim(landed, (b - place) % ratio, 0, keepdims=False)
            for b in range(ratio)
        ],
        axis=1,
    )


def on_device(
    queries,
    key_rows,
    value_rows,
    log_decay,
    init_state,
    attn_gain,
    out_weight,
    residual,
    ffn_gain,
    router,
    expert_ids,
    gate_weight,
    up_weight,
    down_weight,
):
    tokens_here = queries.shape[0]
    heads_here = log_decay.shape[0]
    shaped = (tokens_here, heads_here, HEAD_DIM)
    query_heads = queries.reshape(shaped)
    key_heads = key_rows.reshape(shaped)
    value_heads = value_rows.reshape(shaped)
    upto = jnp.arange(tokens_here)[:, None] >= jnp.arange(tokens_here)[None, :]
    cumulative = jnp.sum(jnp.where(upto[None], log_decay[:, None, :], 0.0), axis=-1)
    block_decay = cumulative[:, -1]
    local_state = block_state(key_heads, value_heads, cumulative)
    prior_decay, prior_state = prior_blocks(block_decay, local_state)
    entering = jnp.exp(prior_decay)[:, None, None] * init_state + prior_state
    attended = block_attend(query_heads, key_heads, value_heads, cumulative, entering)
    inverse = lax.rsqrt(jnp.mean(attended * attended, axis=-1, keepdims=True) + epsilon)
    attn_rows = (
        (attended * inverse * attn_gain.reshape(heads_here, HEAD_DIM))
        .reshape(tokens_here, heads_here * HEAD_DIM)
        .astype(jnp.bfloat16)
    )
    width_here = residual.shape[1]
    first_column = lax.axis_index("head") * width_here
    experts = router.shape[1]
    stream_here = residual.astype(jnp.float32) + project(attn_rows, out_weight).astype(jnp.float32)
    gain_here = lax.dynamic_slice_in_dim(ffn_gain, first_column, width_here, 0)
    router_here = lax.dynamic_slice_in_dim(router, first_column, width_here, 0)
    weighted = stream_here * gain_here
    squares, partial_logits = lax.psum(
        (
            jnp.sum(stream_here * stream_here, axis=-1),
            jnp.dot(weighted, router_here, precision=highest),
        ),
        "head",
    )
    inverse_rms = lax.rsqrt(squares / D + epsilon)[:, None]
    normed = weighted * inverse_rms
    logits = partial_logits * inverse_rms
    expert_in = normed.astype(jnp.bfloat16)
    matches = expert_ids[:, :, None] == jnp.arange(experts)[None, None, :]
    chosen = jnp.sum(jnp.where(matches, logits[:, None, :], 0.0), axis=-1)
    gate_share = jax.nn.sigmoid(chosen - chosen[:, ::-1])
    capacity = 4 * tokens_here // experts
    flat_ids = expert_ids.reshape(-1)
    order = jnp.arange(tokens_here * 2)
    ahead = (flat_ids[None, :] == flat_ids[:, None]) & (order[None, :] < order[:, None])
    position = jnp.sum(ahead.astype(jnp.int32), axis=1)
    slot_index = flat_ids * capacity + position
    target = slot_index[None, :] == jnp.arange(experts * capacity)[:, None]
    source = jnp.sum(jnp.where(target, jnp.arange(tokens_here * 2)[None, :] // 2, 0), axis=1)
    filled = jnp.any(target, axis=1)
    outgoing = jnp.where(filled[:, None], expert_in[source], jnp.zeros((), jnp.bfloat16)).reshape(
        experts, capacity, -1
    )
    gate_here = gate_weight[0]
    up_here = up_weight[0]
    down_here = down_weight[0]
    chunk = capacity // CHUNKS
    arrivals = [
        lax.all_to_all(
            outgoing[:, c * chunk : (c + 1) * chunk],
            "seq",
            split_axis=0,
            concat_axis=0,
            tiled=True,
        )
        for c in range(CHUNKS)
    ]
    results = []
    for arrived in arrivals:
        flat_rows = arrived.reshape(experts * chunk, -1)
        portion = lax.all_gather(flat_rows, "head", axis=1, tiled=True)
        gate_act = jnp.dot(portion, gate_here, preferred_element_type=jnp.float32)
        up_act = jnp.dot(portion, up_here, preferred_element_type=jnp.float32)
        hidden = (jax.nn.silu(gate_act) * up_act).astype(jnp.bfloat16)
        partial_value = jnp.dot(hidden, down_here, preferred_element_type=jnp.float32)
        summed = lax.psum_scatter(
            partial_value.astype(jnp.bfloat16), "head", scatter_dimension=1, tiled=True
        )
        returning = summed.reshape(experts, chunk, -1)
        results.append(
            lax.all_to_all(returning, "seq", split_axis=0, concat_axis=0, tiled=True)
        )
    returned = jnp.concatenate(results, axis=1)
    flat_back = returned.reshape(experts * capacity, -1)
    picked = flat_back[slot_index].reshape(tokens_here, 2, -1).astype(jnp.float32)
    mixture = jnp.sum(gate_share[:, :, None] * picked, axis=1)
    return (stream_here + mixture).astype(jnp.bfloat16)


def solution(mesh):
    return jax.shard_map(
        on_device,
        mesh=mesh,
        in_specs=(
            P("seq", "head"),
            P("seq", "head"),
            P("seq", "head"),
            P("head", "seq"),
            P("head", None, None),
            P("head"),
            P("head", "seq"),
            P("seq", "head"),
            P(),
            P(),
            P("seq", None),
            P("seq", None, "head"),
            P("seq", None, "head"),
            P("seq", "head", None),
        ),
        out_specs=P("seq", "head"),
        check_vma=False,
    )
```

```python
import jax
import jax.numpy as jnp
from jax import lax
from jax.sharding import PartitionSpec as P

D = 6144
HEAD_DIM = 128
CHUNKS = 2


epsilon = 1e-06
highest = lax.Precision.HIGHEST


def prefix(x, axis, combine, identity):
    size, place = (lax.axis_size(axis), lax.axis_index(axis))
    everything = jax.tree.map(
        lambda part, kind: lax.all_gather(part.astype(kind), axis), x, (jnp.bfloat16, jnp.bfloat16)
    )
    start = jax.tree.map(
        lambda part, zero: jnp.broadcast_to(jnp.asarray(zero, part.dtype), part.shape), x, identity
    )

    def turn(k, before):
        reached = k < place
        new = combine(
            before, jax.tree.map(lambda part, own: part[k].astype(own.dtype), everything, x)
        )
        return jax.tree.map(lambda a, b: jnp.where(reached, a, b), new, before)

    return lax.fori_loop(0, size, turn, start)


def block_attend(query_block, key_block, value_block, cumulative, entering):
    length = cumulative.shape[1]
    causal = jnp.arange(length)[:, None] >= jnp.arange(length)[None, :]
    spread = jnp.where(causal[None], cumulative[:, :, None] - cumulative[:, None, :], 0.0)
    fading = jnp.where(causal[None], jnp.exp(spread), 0.0)
    scores = jnp.einsum("thd,shd->hts", query_block, key_block, preferred_element_type=jnp.float32)
    weights = (fading * scores).astype(jnp.bfloat16)
    within = jnp.einsum("hts,shd->thd", weights, value_block, preferred_element_type=jnp.float32)
    carried = jnp.einsum(
        "thd,hde->the", query_block.astype(jnp.float32), entering, precision=highest
    )
    return within + jnp.exp(cumulative).T[:, :, None] * carried


def block_state(key_block, value_block, cumulative):
    remain = jnp.exp(cumulative[:, -1:] - cumulative)
    return jnp.einsum(
        "shd,hs,she->hde",
        key_block.astype(jnp.float32),
        remain,
        value_block.astype(jnp.float32),
        precision=highest,
    )


def join_states(earlier, latter):
    return (earlier[0] + latter[0], jnp.exp(latter[0])[:, None, None] * earlier[1] + latter[1])


def head_sum(partial, axis):
    size, place = (lax.axis_size("head"), lax.axis_index("head"))
    chips, chip, core = (size // 2, place // 2, place % 2)
    width = partial.shape[axis] // size
    swap = [(h, h ^ 1) for h in range(size)]

    def piece(owner):
        return lax.dynamic_slice_in_dim(partial, owner * width, width, axis)

    total = None
    for turn in range(chips - 1, -1, -1):
        to = (chip + turn) % chips
        got = lax.ppermute(piece(2 * to + 1 - core), "head", swap)
        both = piece(2 * to + core).astype(jnp.float32) + got.astype(jnp.float32)
        if turn:
            pairs = [(h, (h + 2 * turn) % size) for h in range(size)]
            both = lax.ppermute(both.astype(jnp.bfloat16), "head", pairs).astype(jnp.float32)
        total = both if total is None else total + both
    return total.astype(jnp.bfloat16)


def project(attn_rows, out_weight):
    seq_size, head_size = (lax.axis_size("seq"), lax.axis_size("head"))
    place = lax.axis_index("seq")
    tokens_here = attn_rows.shape[0]
    ratio = seq_size // head_size
    all_rows = lax.all_gather(attn_rows, "seq", axis=0, tiled=True)
    products = jnp.dot(all_rows, out_weight, preferred_element_type=jnp.float32)
    sums = head_sum(products.astype(jnp.bfloat16), 0).reshape(ratio, tokens_here, -1)
    landed = []
    for turn in range(ratio):
        pairs = [
            (s * head_size + h, (ratio * h + (s + turn) % ratio) * head_size + s // ratio)
            for s in range(seq_size)
            for h in range(head_size)
        ]
        part = lax.dynamic_index_in_dim(sums, (place + turn) % ratio, 0, keepdims=False)
        landed.append(lax.ppermute(part, ("seq", "head"), pairs))
    landed = jnp.stack(landed)
    return jnp.concatenate(
        [
            lax.dynamic_index_in_dim(landed, (place - b) % ratio, 0, keepdims=False)
            for b in range(ratio)
        ],
        axis=1,
    )


def on_device(
    queries,
    key_rows,
    value_rows,
    log_decay,
    init_state,
    attn_gain,
    out_weight,
    residual,
    ffn_gain,
    router,
    expert_ids,
    gate_weight,
    up_weight,
    down_weight,
):
    tokens_here = queries.shape[0]
    heads_here = log_decay.shape[0]
    shaped = (tokens_here, heads_here, HEAD_DIM)
    query_heads = queries.reshape(shaped)
    key_heads = key_rows.reshape(shaped)
    value_heads = value_rows.reshape(shaped)
    upto = jnp.arange(tokens_here)[:, None] >= jnp.arange(tokens_here)[None, :]
    cumulative = jnp.sum(jnp.where(upto[None], log_decay[:, None, :], 0.0), axis=-1)
    block_decay = cumulative[:, -1]
    local_state = block_state(key_heads, value_heads, cumulative)
    identity = (jnp.zeros_like(block_decay), jnp.zeros_like(local_state))
    prior_decay, prior_state = prefix((block_decay, local_state), "seq", join_states, identity)
    entering = jnp.exp(prior_decay)[:, None, None] * init_state + prior_state
    attended = block_attend(query_heads, key_heads, value_heads, cumulative, entering)
    inverse = lax.rsqrt(jnp.mean(attended * attended, axis=-1, keepdims=True) + epsilon)
    attn_rows = (
        (attended * inverse * attn_gain.reshape(heads_here, HEAD_DIM))
        .reshape(tokens_here, heads_here * HEAD_DIM)
        .astype(jnp.bfloat16)
    )
    width_here = residual.shape[1]
    first_column = lax.axis_index("head") * width_here
    experts = router.shape[1]
    stream_here = residual.astype(jnp.float32) + project(attn_rows, out_weight).astype(jnp.float32)
    gain_here = lax.dynamic_slice_in_dim(ffn_gain, first_column, width_here, 0)
    router_here = lax.dynamic_slice_in_dim(router, first_column, width_here, 0)
    weighted = stream_here * gain_here
    squares, partial_logits = lax.psum(
        (
            jnp.sum(stream_here * stream_here, axis=-1),
            jnp.dot(weighted, router_here, precision=highest),
        ),
        "head",
    )
    inverse_rms = lax.rsqrt(squares / D + epsilon)[:, None]
    normed = weighted * inverse_rms
    logits = partial_logits * inverse_rms
    expert_in = normed.astype(jnp.bfloat16)
    matches = expert_ids[:, :, None] == jnp.arange(experts)[None, None, :]
    chosen = jnp.sum(jnp.where(matches, logits[:, None, :], 0.0), axis=-1)
    gate_share = jax.nn.sigmoid(chosen - chosen[:, ::-1])
    capacity = 4 * tokens_here // experts
    flat_ids = expert_ids.reshape(-1)
    order = jnp.arange(tokens_here * 2)
    ahead = (flat_ids[None, :] == flat_ids[:, None]) & (order[None, :] < order[:, None])
    position = jnp.sum(ahead.astype(jnp.int32), axis=1)
    slot_index = flat_ids * capacity + position
    target = slot_index[None, :] == jnp.arange(experts * capacity)[:, None]
    source = jnp.sum(jnp.where(target, jnp.arange(tokens_here * 2)[None, :] // 2, 0), axis=1)
    filled = jnp.any(target, axis=1)
    outgoing = jnp.where(filled[:, None], expert_in[source], jnp.zeros((), jnp.bfloat16)).reshape(
        experts, capacity, -1
    )
    gate_here = gate_weight[0]
    up_here = up_weight[0]
    down_here = down_weight[0]
    chunk = capacity // CHUNKS
    arrivals = [
        lax.all_to_all(
            outgoing[:, c * chunk : (c + 1) * chunk],
            "seq",
            split_axis=0,
            concat_axis=0,
            tiled=True,
        )
        for c in range(CHUNKS)
    ]
    results = []
    for arrived in arrivals:
        flat_rows = arrived.reshape(experts * chunk, -1)
        portion = lax.all_gather(flat_rows, "head", axis=1, tiled=True)
        gate_act = jnp.dot(portion, gate_here, preferred_element_type=jnp.float32)
        up_act = jnp.dot(portion, up_here, preferred_element_type=jnp.float32)
        hidden = (jax.nn.silu(gate_act) * up_act).astype(jnp.bfloat16)
        partial_value = jnp.dot(hidden, down_here, preferred_element_type=jnp.float32)
        summed = head_sum(partial_value.astype(jnp.bfloat16), 1)
        returning = summed.reshape(experts, chunk, -1)
        results.append(
            lax.all_to_all(returning, "seq", split_axis=0, concat_axis=0, tiled=True)
        )
    returned = jnp.concatenate(results, axis=1)
    flat_back = returned.reshape(experts * capacity, -1)
    picked = flat_back[slot_index].reshape(tokens_here, 2, -1).astype(jnp.float32)
    mixture = jnp.sum(gate_share[:, :, None] * picked, axis=1)
    return (stream_here + mixture).astype(jnp.bfloat16)


def solution(mesh):
    return jax.shard_map(
        on_device,
        mesh=mesh,
        in_specs=(
            P("seq", "head"),
            P("seq", "head"),
            P("seq", "head"),
            P("head", "seq"),
            P("head", None, None),
            P("head"),
            P("head", "seq"),
            P("seq", "head"),
            P(),
            P(),
            P("seq", None),
            P("seq", None, "head"),
            P("seq", None, "head"),
            P("seq", "head", None),
        ),
        out_specs=P("seq", "head"),
        check_vma=False,
    )
```
